256 devices in a mesh: dp: 32 (over x, y, core), sp: 8 (over z).
Axes of the slice: x: 4, y: 4, z: 8, core: 2. Of those that a mesh axis runs over, the one named last changes fastest.
Arguments:
- queries: bfloat16 [32768, 4096], P(('dp', 'sp')), may hold values from -45 to 45
- grad_out: bfloat16 [32768, 4096], P(('dp', 'sp')), may hold values from -6 to 6
- key_heads: bfloat16 [32768, 1024], P(('dp', 'sp')), may hold values from -21 to 21
- value_heads: bfloat16 [32768, 1024], P(('dp', 'sp')), may hold values from -6 to 6
- seq_start: int32 [32768], P(('dp', 'sp')), may hold values from 0 to 32640, as said below
Outputs:
- query_grad: bfloat16 [32768, 4096], P(('dp', 'sp'))
- key_grad: bfloat16 [32768, 1024], P(('dp', 'sp'))
- value_grad: bfloat16 [32768, 1024], P(('dp', 'sp'))
The draws below stay inside these ranges and needn't reach their ends.
Inputs may be any that keep to these rules, and one draw needn't show every extreme that they name: seq_start[t] is the first token of the sequence that holds token t. Every sequence starts at a multiple of 128 and is a whole number of 128-token rows; the last 128 tokens form a sequence of their own; every other sequence but the one just before them holds 2048 to 3072 tokens; no sequence touches more than 4 consecutive blocks of 1024 tokens, and in every draw some sequence touches 4.
All inputs are finite; a program needn't handle non-finite values.
Results may differ from the reference program's by a relative error of at most 0.012.
Values may be sent and summed in bfloat16 or wider, within the bound.
No kernel may reach another device: no remote copies, remote signals or barrier semaphores. Data moves between devices by JAX's collectives and lax.ppermute only.
A program may use at most 64 MiB of HBM per device.

```python
import math
import jax
import jax.numpy as jnp
from jax import lax

HQ = 32
HK = 8
HD = 128
UNIT = 128
SPAN = 4
BLK = 1024
TOKENS = 32768


def unit_noise(key):
    return jax.random.truncated_normal(key, -5.0, 5.0, (TOKENS, HK * HD), jnp.float32)


def draw_key_heads(key, part):
    base_noise = unit_noise(key)
    return base_noise.astype(jnp.bfloat16)


def draw_queries(key, part):
    key = jax.random.fold_in(key, 2)
    own_noise = jax.random.truncated_normal(key, -5.0, 5.0, (TOKENS, HQ * HD), jnp.float32)
    return own_noise.astype(jnp.bfloat16)


def draw_seq_start(key, part):
    key = jax.random.fold_in(key, 3)
    unit_block = BLK // UNIT
    unit_count = TOKENS // UNIT
    seq_count = unit_count // (2 * unit_block) + 2
    lengths = jax.random.randint(jax.random.fold_in(key, 11), (seq_count,), 2 * unit_block, 3 * unit_block + 1)
    first_len = jax.random.randint(jax.random.fold_in(key, 12), (), 2 * unit_block + 1, 3 * unit_block)
    lengths = lengths.at[0].set(first_len).at[1].set(3 * unit_block)
    seq_units = jnp.concatenate([jnp.zeros((1,), jnp.int32), jnp.cumsum(lengths).astype(jnp.int32)[:-1]])
    unit_ids = jnp.arange(unit_count, dtype=jnp.int32)
    cut_here = jnp.zeros((unit_count,), bool).at[seq_units].set(True, mode='drop')
    cut_here = cut_here | (unit_ids == 0) | (unit_ids == unit_count - 1)
    start_unit = lax.cummax(jnp.where(cut_here, unit_ids, 0), axis=0)
    token_ids = jnp.arange(TOKENS, dtype=jnp.int32)
    return (start_unit[token_ids // UNIT] * UNIT).astype(jnp.int32)


def level_of(key, shape, pieces, least, high):
    loudness = 1.0
    for axis_at, blocks in pieces:
        heights = jax.random.uniform(jax.random.fold_in(jax.random.fold_in(key, 6), axis_at), (blocks,), jnp.float32, least / len(pieces), high / len(pieces))
        loudness = loudness * jnp.repeat(jnp.exp(heights), shape[axis_at] // blocks).reshape((-1,) + (1,) * (len(shape) - 1 - axis_at))
    return loudness


def gaussian(rng, dims, deviation, reach, shards=(), kind=jnp.bfloat16):
    entries = deviation * jax.random.normal(rng, dims, jnp.float32)
    if shards:
        entries = entries * level_of(rng, dims, shards, -0.22, 0.18)
    return jnp.clip(entries, -reach, reach).astype(kind)


def setup_inputs(seed: int = 0) -> dict:
    splits = jax.random.split(jax.random.key(seed), 6)
    return {
        "queries": draw_queries(jax.random.fold_in(splits[5], 71), 0),
        "grad_out": gaussian(splits[1], (TOKENS, HQ * HD), 1.0, 6.0, ((0, 256),)),
        "key_heads": draw_key_heads(jax.random.fold_in(splits[5], 71), 0),
        "value_heads": gaussian(splits[3], (TOKENS, HK * HD), 1.0, 6.0, ((0, 256),)),
        "seq_start": draw_seq_start(jax.random.fold_in(splits[5], 71), 0),
    }


def group_grads(q_group, o_group, k_window, v_window, visible, score_scale):
    scores = jnp.einsum('igd,jd->gij', q_group, k_window) * score_scale
    scores = jnp.where(visible[None], scores, -jnp.inf)
    row_max = lax.optimization_barrier(jnp.max(scores, axis=-1, keepdims=True))
    log_norm = row_max + jnp.log(lax.optimization_barrier(jnp.sum(jnp.exp(scores - row_max), axis=-1, keepdims=True)))
    weights = jnp.where(visible[None], jnp.exp(scores - log_norm), 0.0)
    slopes = jnp.einsum('igd,jd->gij', o_group, v_window)
    row_dot = lax.optimization_barrier(jnp.sum(weights * slopes, axis=-1, keepdims=True))
    weights_low = lax.optimization_barrier(weights.astype(jnp.bfloat16)).astype(jnp.float32)
    score_grad = lax.optimization_barrier((weights * (slopes - row_dot)).astype(jnp.bfloat16)).astype(jnp.float32)
    dq_part = jnp.einsum('gij,jd->igd', score_grad, k_window) * score_scale
    dk_part = jnp.einsum('gij,igd->jd', score_grad, q_group) * score_scale
    dv_part = jnp.einsum('gij,igd->jd', weights_low, o_group)
    return (dq_part, dk_part, dv_part)

def reference(queries, grad_out, key_heads, value_heads, seq_start):
    score_scale = 1.0 / math.sqrt(HD)
    group_size = HQ // HK
    window = SPAN * BLK
    padding = jnp.zeros(((SPAN - 1) * BLK, HK * HD), jnp.bfloat16)
    keys_padded = jnp.concatenate([padding, key_heads], axis=0)
    values_padded = jnp.concatenate([padding, value_heads], axis=0)
    grad_init = jnp.zeros((TOKENS + (SPAN - 1) * BLK, HK * HD), jnp.float32)

    def one_block(state, block_id):
        dk_total, dv_total = state
        block_first = (block_id * BLK).astype(jnp.int32)
        q_block = lax.dynamic_slice_in_dim(queries, block_first, BLK, 0).astype(jnp.float32).reshape(BLK, HQ, HD)
        o_block = lax.dynamic_slice_in_dim(grad_out, block_first, BLK, 0).astype(jnp.float32).reshape(BLK, HQ, HD)
        k_window = lax.dynamic_slice_in_dim(keys_padded, block_first, window, 0).astype(jnp.float32).reshape(window, HK, HD)
        v_window = lax.dynamic_slice_in_dim(values_padded, block_first, window, 0).astype(jnp.float32).reshape(window, HK, HD)
        starts = lax.dynamic_slice_in_dim(seq_start, block_first, BLK, 0).astype(jnp.int32)
        row_ids = block_first + jnp.arange(BLK, dtype=jnp.int32)
        col_ids = block_first - (SPAN - 1) * BLK + jnp.arange(window, dtype=jnp.int32)
        visible = (col_ids[None, :] >= starts[:, None]) & (col_ids[None, :] <= row_ids[:, None])
        dq_list = []
        dk_list = []
        dv_list = []
        for head_kv in range(HK):
            lower = head_kv * group_size
            dq_part, dk_part, dv_part = group_grads(q_block[:, lower:lower + group_size, :], o_block[:, lower:lower + group_size, :], k_window[:, head_kv, :], v_window[:, head_kv, :], visible, score_scale)
            dq_list.append(dq_part)
            dk_list.append(dk_part)
            dv_list.append(dv_part)
        dq_block = jnp.concatenate(dq_list, axis=1).reshape(BLK, HQ * HD).astype(jnp.bfloat16)
        dk_window = jnp.stack(dk_list, axis=1).reshape(window, HK * HD)
        dv_window = jnp.stack(dv_list, axis=1).reshape(window, HK * HD)
        dk_total = lax.dynamic_update_slice_in_dim(dk_total, lax.dynamic_slice_in_dim(dk_total, block_first, window, 0) + dk_window, block_first, 0)
        dv_total = lax.dynamic_update_slice_in_dim(dv_total, lax.dynamic_slice_in_dim(dv_total, block_first, window, 0) + dv_window, block_first, 0)
        return ((dk_total, dv_total), dq_block)
    (dk_total, dv_total), dq_blocks = lax.scan(one_block, (grad_init, grad_init), jnp.arange(TOKENS // BLK, dtype=jnp.int32))
    query_grad = dq_blocks.reshape(TOKENS, HQ * HD)
    key_grad = dk_total[(SPAN - 1) * BLK:].astype(jnp.bfloat16)
    value_grad = dv_total[(SPAN - 1) * BLK:].astype(jnp.bfloat16)
    return (query_grad, key_grad, value_grad)
```

```python
import functools
import math

import jax
import jax.numpy as jnp
from jax import lax
from jax.experimental import pallas as pl
from jax.experimental.pallas import tpu as pltpu
from jax.sharding import PartitionSpec as P

HQ = 32
HK = 8
HD = 128
UNIT = 128
SPAN = 4
BLK = 1024
PAST = (SPAN - 1) * BLK
GROUP = HQ // HK
PARTS = 2
HEADS = GROUP // PARTS
LANES = HEADS * UNIT
CHUNK = 512
ROWS = SPAN * BLK + CHUNK
SCALE = 1.0 / math.sqrt(HD)
SCALE2 = SCALE * math.log2(math.e)
FILL = -1e30
BF, F32 = jnp.bfloat16, jnp.float32


def dot(a, b, ca, cb):
    return lax.dot_general(a, b, (((ca,), (cb,)), ((), ())), preferred_element_type=F32)


def fold(tile, reduce):
    return reduce(tile.reshape(CHUNK // 8, 8, LANES), axis=0)


def attention_kernel(last, first_ref, qo_ref, h3_ref, h2_ref, h1_ref, own_ref, *refs):
    if last:
        sum_in, refs = refs[:2], refs[2:]
    dq_ref, *refs = refs
    outs, (kbuf, vbuf, ebuf, pbuf, dkacc, dvacc, dqacc) = refs[:-7], refs[-7:]
    for at, ref in enumerate((h3_ref, h2_ref, h1_ref)):
        kbuf[at * BLK : (at + 1) * BLK, :] = ref[:, :HD]
        vbuf[at * BLK : (at + 1) * BLK, :] = ref[:, HD:]
    for z in range(BLK // UNIT):
        low = PAST + z * UNIT
        kbuf[low : low + UNIT, :] = own_ref[z, :UNIT, :HD]
        vbuf[low : low + UNIT, :] = own_ref[z, :UNIT, HD:]
    kbuf[SPAN * BLK :, :] = jnp.zeros((CHUNK, HD), BF)
    vbuf[SPAN * BLK :, :] = jnp.zeros((CHUNK, HD), BF)
    if last:
        dkacc[: SPAN * BLK, :] = sum_in[0][...]
        dvacc[: SPAN * BLK, :] = sum_in[1][...]
        dkacc[SPAN * BLK :, :] = jnp.zeros((CHUNK, HD), F32)
        dvacc[SPAN * BLK :, :] = jnp.zeros((CHUNK, HD), F32)
    else:
        dkacc[...] = jnp.zeros_like(dkacc)
        dvacc[...] = jnp.zeros_like(dvacc)

    def row_step(t, _):
        row = pl.multiple_of(t * UNIT, UNIT)
        rows = pl.ds(row, UNIT)
        q_t = jnp.concatenate([qo_ref[rows, h * HD : (h + 1) * HD] for h in range(HEADS)], axis=0)
        o_t = jnp.concatenate(
            [qo_ref[rows, (HEADS + h) * HD : (HEADS + h + 1) * HD] for h in range(HEADS)], axis=0
        )
        first = first_ref[t]
        count = (PAST + row + UNIT - first + CHUNK - 1) // CHUNK

        def keys(i):
            return pl.ds(pl.multiple_of(first + i * CHUNK, UNIT), CHUNK)

        def slot(i):
            return pl.ds(pl.multiple_of(i * CHUNK, CHUNK), CHUNK)

        def scores(i, top, masked):
            s = dot(kbuf[keys(i), :], q_t, 1, 1)
            if masked:
                key_id = first + i * CHUNK + lax.broadcasted_iota(jnp.int32, (CHUNK, LANES), 0)
                query_id = PAST + row + (
                    lax.broadcasted_iota(jnp.int32, (CHUNK, LANES), 1) & (UNIT - 1)
                )
                s = jnp.where(key_id <= query_id, s, FILL)
            ebuf[slot(i), :] = s
            return jnp.maximum(top, fold(s, jnp.max))

        top = lax.fori_loop(
            0, count - 1, lambda i, m: scores(i, m, False), jnp.full((8, LANES), FILL, F32)
        )
        top = scores(count - 1, top, True)
        top = jnp.max(top, axis=0, keepdims=True) * SCALE2

        def sums(i, carry):
            total, weighted = carry
            e = jnp.exp2(ebuf[slot(i), :] * SCALE2 - top)
            ebuf[slot(i), :] = e
            slopes = dot(vbuf[keys(i), :], o_t, 1, 1)
            pbuf[slot(i), :] = slopes
            return total + fold(e, jnp.sum), weighted + fold(e * slopes, jnp.sum)

        zero = jnp.zeros((8, LANES), F32)
        total, weighted = lax.fori_loop(0, count, sums, (zero, zero))
        inverse = 1.0 / jnp.sum(total, axis=0, keepdims=True)
        row_dot = jnp.sum(weighted, axis=0, keepdims=True) * inverse
        dqacc[...] = jnp.zeros_like(dqacc)

        def grads(i, _):
            w = ebuf[slot(i), :] * inverse
            ds = (w * (pbuf[slot(i), :] - row_dot)).astype(BF)
            at = keys(i)
            dvacc[at, :] += dot(w.astype(BF), o_t, 1, 0)
            dkacc[at, :] += dot(ds, q_t, 1, 0)
            dqacc[...] += dot(kbuf[at, :], ds, 0, 0)
            return 0

        lax.fori_loop(0, count, grads, 0)
        for h in range(HEADS):
            dq = dqacc[:, h * HD : (h + 1) * HD].T * SCALE
            dq_ref[rows, h * HD : (h + 1) * HD] = dq.astype(BF)
        return 0

    lax.fori_loop(0, BLK // UNIT, row_step, 0)
    if last:
        for at, out in enumerate(outs):
            low = at * BLK
            scaled = dkacc[low : low + BLK, :] * SCALE
            out[:, :HD] = scaled.astype(out.dtype)
            out[:, HD:] = dvacc[low : low + BLK, :].astype(out.dtype)
    else:
        outs[0][...] = dkacc[: SPAN * BLK, :]
        outs[1][...] = dvacc[: SPAN * BLK, :]


def attend(first, qo, halo, own, sums=()):
    last = bool(sums)
    vmem = pl.BlockSpec(memory_space=pltpu.VMEM)
    shape = jax.ShapeDtypeStruct
    if last:
        outs = (shape((BLK, 2 * HD), BF),) * 3 + (shape((BLK, 2 * HD), F32),)
    else:
        outs = (shape((SPAN * BLK, HD), F32),) * 2
    outs = (shape((BLK, HEADS * HD), BF),) + outs
    return pl.pallas_call(
        functools.partial(attention_kernel, last),
        out_shape=outs,
        in_specs=[pl.BlockSpec(memory_space=pltpu.SMEM)] + [vmem] * (5 + len(sums)),
        out_specs=(vmem,) * len(outs),
        scratch_shapes=[
            pltpu.VMEM((ROWS, HD), BF),
            pltpu.VMEM((ROWS, HD), BF),
            pltpu.VMEM((ROWS, LANES), F32),
            pltpu.VMEM((ROWS, LANES), F32),
            pltpu.VMEM((ROWS, HD), F32),
            pltpu.VMEM((ROWS, HD), F32),
            pltpu.VMEM((HD, LANES), F32),
        ],
        compiler_params=pltpu.CompilerParams(vmem_limit_bytes=50 << 20),
        cost_estimate=pl.CostEstimate(
            flops=20_000_000_000, bytes_accessed=12 << 20, transcendentals=0
        ),
    )(first, qo, *halo, own, *sums)


def shifted(block, by):
    peers = lax.axis_size("dp")
    pairs = [(i, i + by) for i in range(peers) if 0 <= i + by < peers]
    return lax.ppermute(block, "dp", pairs)


def exchanged(block):
    return lax.ppermute(block, "dp", [(i, i ^ 1) for i in range(lax.axis_size("dp"))])


def all_to_all(array):
    return lax.all_to_all(array, "sp", split_axis=0, concat_axis=0, tiled=True)


def on_device(queries, grad_out, key_heads, value_heads, seq_start):
    even = lax.axis_index("dp") % 2 == 0
    window_first = lax.axis_index("dp") * BLK - PAST
    by_head = lambda a: a.reshape(UNIT, HK, -1).transpose(1, 0, 2)
    start = jnp.broadcast_to((seq_start[0] // UNIT).astype(BF), (HK, 16, 2 * HD))
    kv = jnp.concatenate([by_head(key_heads), by_head(value_heads)], axis=2)
    own = all_to_all(jnp.concatenate([kv, start], axis=1))
    first = own[:, UNIT, 0].astype(F32).astype(jnp.int32) * UNIT - window_first
    block = own[:, :UNIT].reshape(BLK, 2 * HD)
    h1 = shifted(block, 1)
    h3 = shifted(block, 3)
    h2 = exchanged(jnp.where(even, h1, h3))
    q_parts = queries.reshape(UNIT, HK, PARTS, HEADS * HD)
    o_parts = grad_out.reshape(UNIT, HK, PARTS, HEADS * HD)
    dq, sums = [], ()
    for part in range(PARTS):
        qo = jnp.concatenate([q_parts[:, :, part], o_parts[:, :, part]], axis=2).transpose(1, 0, 2)
        qo = all_to_all(qo).reshape(BLK, 2 * HEADS * HD)
        dq_part, *sums = attend(first, qo, (h3, h2, h1), own, sums)
        dq.append(all_to_all(dq_part.reshape(HK, UNIT, HEADS * HD)))
    p3, p2, p1, mine = sums
    swap = exchanged(p2).astype(F32)
    t1 = (p1.astype(F32) + jnp.where(even, swap, 0.0)).astype(BF)
    t3 = (p3.astype(F32) + jnp.where(even, 0.0, swap)).astype(BF)
    total = mine + shifted(t1, -1).astype(F32) + shifted(t3, -3).astype(F32)
    dkv = all_to_all(total.astype(BF).reshape(HK, UNIT, 2 * HD))
    dkv = dkv.transpose(1, 0, 2)
    query_grad = jnp.concatenate(dq, axis=2).transpose(1, 0, 2).reshape(UNIT, HQ * HD)
    key_grad = dkv[:, :, :HD].reshape(UNIT, HK * HD)
    value_grad = dkv[:, :, HD:].reshape(UNIT, HK * HD)
    return (query_grad, key_grad, value_grad)


def solution(mesh):
    rows = P(("dp", "sp"), None)
    return jax.shard_map(
        on_device,
        mesh=mesh,
        in_specs=(rows, rows, rows, rows, P(("dp", "sp"))),
        out_specs=(rows, rows, rows),
        check_vma=False,
    )
```

```python
import functools
import math

import jax
import jax.numpy as jnp
from jax import lax
from jax.experimental import pallas as pl
from jax.experimental.pallas import tpu as pltpu
from jax.sharding import PartitionSpec as P

HQ = 32
HK = 8
HD = 128
UNIT = 128
SPAN = 4
BLK = 1024
UNITS = BLK // UNIT
STEPS = ((2, 1, 0, -1), (-2, -3, 4, 3))
PAST = (SPAN - 1) * BLK
HEADS = HQ // HK
TILE = 256
LANES = HEADS * TILE
CHUNK = 512
ROWS = SPAN * BLK + CHUNK
SCALE = 1.0 / math.sqrt(HD)
SCALE2 = SCALE * math.log2(math.e)
FILL = -1e30
BF, F32 = jnp.bfloat16, jnp.float32


def dot(a, b, ca, cb):
    return lax.dot_general(a, b, (((ca,), (cb,)), ((), ())), preferred_element_type=F32)


def fold(tile, reduce):
    return reduce(tile.reshape(CHUNK // 8, 8, LANES), axis=0)


def attention_kernel(last, info_ref, *refs):
    pieces, blocks, refs = refs[:4], refs[4:8], refs[8:]
    if last:
        sums, refs = refs[:2], refs[2:]
    dq_refs, refs = refs[:4], refs[4:]
    outs, refs = (refs[:4], refs[4:]) if last else (refs[:2], refs[2:])
    kbuf, vbuf, ebuf, pbuf, mbuf, dkacc, dvacc, dqacc, qobuf, dqbuf, in_sem, out_sem, *wide = refs
    loads = [(piece, qobuf.at[m]) for m, piece in enumerate(pieces)]
    for at, block in enumerate(blocks):
        rows = pl.ds(at * BLK, BLK)
        loads.append((block.at[:, pl.ds(0, HD)], kbuf.at[rows, :]))
        loads.append((block.at[:, pl.ds(HD, HD)], vbuf.at[rows, :]))
    if last:
        loads += [(sums[0], dkacc), (sums[1], dvacc)]
    loads = [pltpu.make_async_copy(a, b, in_sem.at[n]) for n, (a, b) in enumerate(loads)]
    for copy in loads:
        copy.start()
    kbuf[SPAN * BLK :, :] = jnp.zeros((CHUNK, HD), BF)
    vbuf[SPAN * BLK :, :] = jnp.zeros((CHUNK, HD), BF)
    if not last:
        dkacc[...] = jnp.zeros_like(dkacc)
        dvacc[...] = jnp.zeros_like(dvacc)
    for copy in loads:
        copy.wait()
    lane = lax.broadcasted_iota(jnp.int32, (1, LANES), 1) & (TILE - 1)

    def tile_step(pair, _):
        entry = UNITS + 8 * last + 4 * pair
        place = [info_ref[entry + 2 * n] for n in range(2)]
        unit = [info_ref[entry + 2 * n + 1] for n in range(2)]
        side = lambda low: jnp.concatenate(
            [
                qobuf[place[n], :, low + h * HD : low + (h + 1) * HD]
                for h in range(HEADS)
                for n in range(2)
            ],
            axis=0,
        )
        q_t, o_t = side(0), side(HEADS * HD)
        begin = [info_ref[u] for u in unit]
        row = [PAST + u * UNIT for u in unit]
        first = jnp.minimum(begin[0], begin[1])
        starts = jnp.where(lane < UNIT, begin[0], begin[1])
        query_id = jnp.where(lane < UNIT, row[0] + lane, row[1] + lane - UNIT)
        same = begin[0] == begin[1]
        plain = jnp.where(same, (jnp.minimum(row[0], row[1]) - first) // CHUNK, 0)
        count = (jnp.maximum(row[0], row[1]) + UNIT - first + CHUNK - 1) // CHUNK

        def keys(i):
            return pl.ds(pl.multiple_of(first + i * CHUNK, UNIT), CHUNK)

        def slot(i):
            return pl.ds(pl.multiple_of(i * CHUNK, CHUNK), CHUNK)

        def forward(masked, i, carry):
            top, total, weighted = carry
            at = keys(i)
            s = dot(kbuf[at, :], q_t, 1, 1)
            if masked:
                key_id = first + i * CHUNK + lax.broadcasted_iota(jnp.int32, (CHUNK, LANES), 0)
                s = jnp.where((key_id <= query_id) & (key_id >= starts), s, FILL)
            slopes = dot(vbuf[at, :], o_t, 1, 1)
            new = jnp.maximum(top, jnp.max(fold(s, jnp.max), axis=0, keepdims=True) * SCALE2)
            e = jnp.exp2(s * SCALE2 - new)
            ebuf[slot(i), :] = e
            pbuf[slot(i), :] = slopes
            mbuf[pl.ds(i, 1), :] = new
            shrink = jnp.exp2(top - new)
            total = total * shrink + fold(e, jnp.sum)
            return new, total, weighted * shrink + fold(e * slopes, jnp.sum)

        zero = jnp.zeros((8, LANES), F32)
        carry = (jnp.full((1, LANES), FILL, F32), zero, zero)
        plainly = functools.partial(forward, False)
        twice = lambda i, c: plainly(2 * i + 1, plainly(2 * i, c))
        carry = lax.fori_loop(0, plain // 2, twice, carry)
        carry = lax.fori_loop(plain // 2 * 2, plain, plainly, carry)
        top, total, weighted = lax.fori_loop(
            plain, count, functools.partial(forward, True), carry
        )
        inverse = 1.0 / jnp.sum(total, axis=0, keepdims=True)
        row_dot = jnp.sum(weighted, axis=0, keepdims=True) * inverse
        dqacc[...] = jnp.zeros_like(dqacc)

        def grads(i, _):
            w = ebuf[slot(i), :] * (jnp.exp2(mbuf[pl.ds(i, 1), :] - top) * inverse)
            ds = (w * (pbuf[slot(i), :] - row_dot)).astype(BF)
            at = keys(i)
            dvacc[at, :] += dot(w.astype(BF), o_t, 1, 0)
            dkacc[at, :] += dot(ds, q_t, 1, 0)
            dqacc[...] += dot(kbuf[at, :], ds, 0, 0)
            return 0

        def two_grads(i, _):
            grads(2 * i, 0)
            return grads(2 * i + 1, 0)

        lax.fori_loop(0, count // 2, two_grads, 0)
        lax.fori_loop(count // 2 * 2, count, grads, 0)
        for h in range(HEADS):
            dq = (dqacc[:, h * TILE : (h + 1) * TILE].T * SCALE).astype(BF)
            for n in range(2):
                dqbuf[place[n], :, h * HD : (h + 1) * HD] = dq[n * UNIT : (n + 1) * UNIT]
        return 0

    lax.fori_loop(0, 2, tile_step, 0)
    stores = []

    def store(a, b):
        stores.append(pltpu.make_async_copy(a, b, out_sem.at[len(stores)]))
        stores[-1].start()

    for m, out in enumerate(dq_refs):
        store(dqbuf.at[m], out)
    if last:
        for at, (held, out) in enumerate(zip(wide, outs)):
            low = at * BLK
            held[:, :HD] = (dkacc[low : low + BLK, :] * SCALE).astype(out.dtype)
            held[:, HD:] = dvacc[low : low + BLK, :].astype(out.dtype)
            store(held, out)
    else:
        store(dkacc, outs[0])
        store(dvacc, outs[1])
    for copy in stores:
        copy.wait()


def attend(last, info, pieces, blocks, sums=()):
    hbm = pl.BlockSpec(memory_space=pl.ANY)
    shape = jax.ShapeDtypeStruct
    scratch = [
        pltpu.VMEM((ROWS, HD), BF),
        pltpu.VMEM((ROWS, HD), BF),
        pltpu.VMEM((ROWS, LANES), F32),
        pltpu.VMEM((ROWS, LANES), F32),
        pltpu.VMEM((16, LANES), F32),
        pltpu.VMEM((ROWS, HD), F32),
        pltpu.VMEM((ROWS, HD), F32),
        pltpu.VMEM((HD, LANES), F32),
        pltpu.VMEM((4, UNIT, 2 * HEADS * HD), BF),
        pltpu.VMEM((4, UNIT, HEADS * HD), BF),
        pltpu.SemaphoreType.DMA((14,)),
        pltpu.SemaphoreType.DMA((8,)),
    ]
    if last:
        wide = ((BLK, 2 * HD), BF), ((BLK, 2 * HD), BF), ((BLK, 2 * HD), BF), ((BLK, 2 * HD), F32)
        scratch += [pltpu.VMEM(*w) for w in wide]
    else:
        wide = (((ROWS, HD), F32),) * 2
    outs = (shape((UNIT, HEADS * HD), BF),) * 4 + tuple(shape(*w) for w in wide)
    return pl.pallas_call(
        functools.partial(attention_kernel, last),
        out_shape=outs,
        in_specs=[pl.BlockSpec(memory_space=pltpu.SMEM)] + [hbm] * (8 + len(sums)),
        out_specs=(hbm,) * len(outs),
        scratch_shapes=scratch,
        compiler_params=pltpu.CompilerParams(vmem_limit_bytes=58 << 20),
        cost_estimate=pl.CostEstimate(
            flops=14_000_000_000, bytes_accessed=12 << 20, transcendentals=0
        ),
    )(info, *pieces, *blocks, *sums)


def shifted(block, by):
    peers = lax.axis_size("dp")
    pairs = [(i, i + by) for i in range(peers) if 0 <= i + by < peers]
    return lax.ppermute(block, "dp", pairs)


def exchanged(block):
    return lax.ppermute(block, "dp", [(i, i ^ 1) for i in range(lax.axis_size("dp"))])


def target(index, step):
    if abs(step) == 2 and index % 2:
        step = -step
    return (index + step) % UNITS


def round_by(block, step, back=False):
    if step == 0:
        return block
    pairs = [(i, target(i, step)) for i in range(UNITS)]
    return lax.ppermute(block, "sp", [(b, a) for a, b in pairs] if back else pairs)


def tables():
    sent = [{s: target(me, s) for s in STEPS[0] + STEPS[1]} for me in range(UNITS)]
    placed = []
    for me in range(UNITS):
        row = []
        for steps in STEPS:
            source = [next(i for i in range(UNITS) if target(i, s) == me) for s in steps]
            order = (0, 1, 2, 3) if me % 2 == 0 else (1, 2, 3, 0)
            for n in order:
                row += [n, source[n]]
        placed.append(row)
    return sent, placed


def all_to_all(array):
    return lax.all_to_all(array, "sp", split_axis=0, concat_axis=0, tiled=True)


def on_device(queries, grad_out, key_heads, value_heads, seq_start):
    even = lax.axis_index("dp") % 2 == 0
    window_first = lax.axis_index("dp") * BLK - PAST
    me = lax.axis_index("sp")
    by_head = lambda a: a.reshape(UNIT, HK, -1)
    sent, placed = tables()
    goes = {
        s: jnp.array([row[s] for row in sent], jnp.int32)[me] * HEADS * HD for s in sent[0]
    }
    part_of = lambda a, s: lax.dynamic_slice_in_dim(a, goes[s], HEADS * HD, 1)
    start = jnp.broadcast_to((seq_start[0] // UNIT).astype(BF), (HK, 16, 2 * HD))
    kv = jnp.concatenate([by_head(key_heads), by_head(value_heads)], axis=2).transpose(1, 0, 2)
    own = all_to_all(jnp.concatenate([kv, start], axis=1))
    units = {
        s: round_by(jnp.concatenate([part_of(queries, s), part_of(grad_out, s)], axis=1), s)
        for s in STEPS[0] + STEPS[1]
    }
    info = own[:, UNIT, 0].astype(F32).astype(jnp.int32) * UNIT - window_first
    info = jnp.concatenate([info, jnp.array(placed, jnp.int32)[me]])
    block = own[:, :UNIT].reshape(BLK, 2 * HD)
    h1 = shifted(block, 1)
    h3 = shifted(block, 3)
    near = [units[s] for s in STEPS[0]]
    h1, h3, *near = lax.optimization_barrier((h1, h3, *near))
    units.update(zip(STEPS[0], near))
    h2 = exchanged(jnp.where(even, h1, h3))
    grads, sums = {}, ()
    for last in (False, True):
        pieces = [units[s] for s in STEPS[last]]
        result = attend(last, info, pieces, (h3, h2, h1, block), sums)
        dq, sums = result[:4], result[4:]
        grads.update({s: round_by(piece, s, True) for s, piece in zip(STEPS[last], dq)})
    p3, p2, p1, mine = sums
    early = [grads[s] for s in STEPS[0]]
    p2, *early = lax.optimization_barrier((p2, *early))
    grads.update(zip(STEPS[0], early))
    swap = exchanged(p2).astype(F32)
    t1 = (p1.astype(F32) + jnp.where(even, swap, 0.0)).astype(BF)
    t3 = (p3.astype(F32) + jnp.where(even, 0.0, swap)).astype(BF)
    total = mine + shifted(t1, -1).astype(F32) + shifted(t3, -3).astype(F32)
    dkv = all_to_all(total.astype(BF).reshape(UNITS, UNIT, 2 * HD)).transpose(1, 0, 2)
    query_grad = jnp.zeros((UNIT, HQ * HD), BF)
    for s, piece in grads.items():
        query_grad = lax.dynamic_update_slice_in_dim(query_grad, piece, goes[s], 1)
    key_grad = dkv[:, :, :HD].reshape(UNIT, HK * HD)
    value_grad = dkv[:, :, HD:].reshape(UNIT, HK * HD)
    return (query_grad, key_grad, value_grad)


def solution(mesh):
    rows = P(("dp", "sp"), None)
    return jax.shard_map(
        on_device,
        mesh=mesh,
        in_specs=(rows, rows, rows, rows, P(("dp", "sp"))),
        out_specs=(rows, rows, rows),
        check_vma=False,
    )
```

```python
import functools
import math

import jax
import jax.numpy as jnp
from jax import lax
from jax.experimental import pallas as pl
from jax.experimental.pallas import tpu as pltpu
from jax.sharding import PartitionSpec as P

HQ = 32
HK = 8
HD = 128
UNIT = 128
SPAN = 4
BLK = 1024
UNITS = BLK // UNIT
STEPS = ((2, 1, 0, -1), (-2, -3, 4, 3))
PAST = (SPAN - 1) * BLK
HEADS = HQ // HK
TILE = 256
LANES = HEADS * TILE
CHUNK = 512
ROWS = SPAN * BLK + CHUNK
SCALE = 1.0 / math.sqrt(HD)
SCALE2 = SCALE * math.log2(math.e)
FILL = -1e30
BF, F32 = jnp.bfloat16, jnp.float32


def dot(a, b, ca, cb):
    return lax.dot_general(a, b, (((ca,), (cb,)), ((), ())), preferred_element_type=F32)


def fold(tile, reduce):
    return reduce(tile.reshape(CHUNK // 8, 8, LANES), axis=0)


def attention_kernel(last, info_ref, *refs):
    pieces, blocks, refs = refs[:4], refs[4:8], refs[8:]
    if last:
        sums, refs = refs[:2], refs[2:]
    dq_refs, refs = refs[:4], refs[4:]
    outs, refs = (refs[:4], refs[4:]) if last else (refs[:2], refs[2:])
    kbuf, vbuf, ebuf, pbuf, mbuf, dkacc, dvacc, dqacc, qobuf, dqbuf, in_sem, out_sem, *wide = refs
    loads = [(piece, qobuf.at[m]) for m, piece in enumerate(pieces)]
    for at, block in enumerate(blocks):
        rows = pl.ds(at * BLK, BLK)
        loads.append((block.at[:, pl.ds(0, HD)], kbuf.at[rows, :]))
        loads.append((block.at[:, pl.ds(HD, HD)], vbuf.at[rows, :]))
    late = len(loads)
    if last:
        *wide, sum_k, sum_v = wide
        loads += [(sums[0], sum_k), (sums[1], sum_v)]
    loads = [pltpu.make_async_copy(a, b, in_sem.at[n]) for n, (a, b) in enumerate(loads)]
    for copy in loads:
        copy.start()
    kbuf[SPAN * BLK :, :] = jnp.zeros((CHUNK, HD), BF)
    vbuf[SPAN * BLK :, :] = jnp.zeros((CHUNK, HD), BF)
    dkacc[...] = jnp.zeros_like(dkacc)
    dvacc[...] = jnp.zeros_like(dvacc)
    for copy in loads[:late]:
        copy.wait()
    lane = lax.broadcasted_iota(jnp.int32, (1, LANES), 1) & (TILE - 1)

    def tile_step(pair, _):
        entry = UNITS + 8 * last + 4 * pair
        place = [info_ref[entry + 2 * n] for n in range(2)]
        unit = [info_ref[entry + 2 * n + 1] for n in range(2)]
        side = lambda low: jnp.concatenate(
            [
                qobuf[place[n], :, low + h * HD : low + (h + 1) * HD]
                for h in range(HEADS)
                for n in range(2)
            ],
            axis=0,
        )
        q_t, o_t = side(0), side(HEADS * HD)
        begin = [info_ref[u] for u in unit]
        row = [PAST + u * UNIT for u in unit]
        first = jnp.minimum(begin[0], begin[1])
        starts = jnp.where(lane < UNIT, begin[0], begin[1])
        query_id = jnp.where(lane < UNIT, row[0] + lane, row[1] + lane - UNIT)
        same = begin[0] == begin[1]
        plain = jnp.where(same, (jnp.minimum(row[0], row[1]) - first) // CHUNK, 0)
        count = (jnp.maximum(row[0], row[1]) + UNIT - first + CHUNK - 1) // CHUNK

        def keys(i):
            return pl.ds(pl.multiple_of(first + i * CHUNK, UNIT), CHUNK)

        def slot(i):
            return pl.ds(pl.multiple_of(i * CHUNK, CHUNK), CHUNK)

        def forward(masked, i, carry):
            top, total, weighted = carry
            at = keys(i)
            s = dot(kbuf[at, :], q_t, 1, 1)
            if masked:
                key_id = first + i * CHUNK + lax.broadcasted_iota(jnp.int32, (CHUNK, LANES), 0)
                s = jnp.where((key_id <= query_id) & (key_id >= starts), s, FILL)
            slopes = dot(vbuf[at, :], o_t, 1, 1)
            new = jnp.maximum(top, jnp.max(fold(s, jnp.max), axis=0, keepdims=True) * SCALE2)
            e = jnp.exp2(s * SCALE2 - new)
            ebuf[slot(i), :] = e
            pbuf[slot(i), :] = slopes
            mbuf[pl.ds(i, 1), :] = new
            shrink = jnp.exp2(top - new)
            total = total * shrink + fold(e, jnp.sum)
            return new, total, weighted * shrink + fold(e * slopes, jnp.sum)

        zero = jnp.zeros((8, LANES), F32)
        carry = (jnp.full((1, LANES), FILL, F32), zero, zero)
        plainly = functools.partial(forward, False)
        twice = lambda i, c: plainly(2 * i + 1, plainly(2 * i, c))
        carry = lax.fori_loop(0, plain // 2, twice, carry)
        carry = lax.fori_loop(plain // 2 * 2, plain, plainly, carry)
        top, total, weighted = lax.fori_loop(
            plain, count, functools.partial(forward, True), carry
        )
        inverse = 1.0 / jnp.sum(total, axis=0, keepdims=True)
        row_dot = jnp.sum(weighted, axis=0, keepdims=True) * inverse
        dqacc[...] = jnp.zeros_like(dqacc)

        def grads(i, _):
            w = ebuf[slot(i), :] * (jnp.exp2(mbuf[pl.ds(i, 1), :] - top) * inverse)
            ds = (w * (pbuf[slot(i), :] - row_dot)).astype(BF)
            at = keys(i)
            dvacc[at, :] += dot(w.astype(BF), o_t, 1, 0)
            dkacc[at, :] += dot(ds, q_t, 1, 0)
            dqacc[...] += dot(kbuf[at, :], ds, 0, 0)
            return 0

        def two_grads(i, _):
            grads(2 * i, 0)
            return grads(2 * i + 1, 0)

        lax.fori_loop(0, count // 2, two_grads, 0)
        lax.fori_loop(count // 2 * 2, count, grads, 0)
        for h in range(HEADS):
            dq = (dqacc[:, h * TILE : (h + 1) * TILE].T * SCALE).astype(BF)
            for n in range(2):
                dqbuf[place[n], :, h * HD : (h + 1) * HD] = dq[n * UNIT : (n + 1) * UNIT]
        return 0

    lax.fori_loop(0, 2, tile_step, 0)
    stores = []

    def store(a, b):
        stores.append(pltpu.make_async_copy(a, b, out_sem.at[len(stores)]))
        stores[-1].start()

    for m, out in enumerate(dq_refs):
        store(dqbuf.at[m], out)
    if last:
        for copy in loads[late:]:
            copy.wait()
        for at, (held, out) in enumerate(zip(wide, outs)):
            here = slice(at * BLK, (at + 1) * BLK)
            held[:, :HD] = ((dkacc[here, :] + sum_k[here, :]) * SCALE).astype(out.dtype)
            held[:, HD:] = (dvacc[here, :] + sum_v[here, :]).astype(out.dtype)
            store(held, out)
    else:
        store(dkacc, outs[0])
        store(dvacc, outs[1])
    for copy in stores:
        copy.wait()


def attend(last, info, pieces, blocks, sums=()):
    hbm = pl.BlockSpec(memory_space=pl.ANY)
    shape = jax.ShapeDtypeStruct
    scratch = [
        pltpu.VMEM((ROWS, HD), BF),
        pltpu.VMEM((ROWS, HD), BF),
        pltpu.VMEM((ROWS, LANES), F32),
        pltpu.VMEM((ROWS, LANES), F32),
        pltpu.VMEM((16, LANES), F32),
        pltpu.VMEM((ROWS, HD), F32),
        pltpu.VMEM((ROWS, HD), F32),
        pltpu.VMEM((HD, LANES), F32),
        pltpu.VMEM((4, UNIT, 2 * HEADS * HD), BF),
        pltpu.VMEM((4, UNIT, HEADS * HD), BF),
        pltpu.SemaphoreType.DMA((14,)),
        pltpu.SemaphoreType.DMA((8,)),
    ]
    if last:
        wide = ((BLK, 2 * HD), BF), ((BLK, 2 * HD), BF), ((BLK, 2 * HD), BF), ((BLK, 2 * HD), F32)
        scratch += [pltpu.VMEM(*w) for w in wide] + [pltpu.VMEM((ROWS, HD), F32)] * 2
    else:
        wide = (((ROWS, HD), F32),) * 2
    outs = (shape((UNIT, HEADS * HD), BF),) * 4 + tuple(shape(*w) for w in wide)
    return pl.pallas_call(
        functools.partial(attention_kernel, last),
        out_shape=outs,
        in_specs=[pl.BlockSpec(memory_space=pltpu.SMEM)] + [hbm] * (8 + len(sums)),
        out_specs=(hbm,) * len(outs),
        scratch_shapes=scratch,
        compiler_params=pltpu.CompilerParams(vmem_limit_bytes=60 << 20),
        cost_estimate=pl.CostEstimate(
            flops=14_000_000_000, bytes_accessed=12 << 20, transcendentals=0
        ),
    )(info, *pieces, *blocks, *sums)


def shifted(block, by):
    peers = lax.axis_size("dp")
    pairs = [(i, i + by) for i in range(peers) if 0 <= i + by < peers]
    return lax.ppermute(block, "dp", pairs)


def exchanged(block):
    return lax.ppermute(block, "dp", [(i, i ^ 1) for i in range(lax.axis_size("dp"))])


def target(index, step):
    if abs(step) == 2 and index % 2:
        step = -step
    return (index + step) % UNITS


def round_by(block, step, back=False):
    if step == 0:
        return block
    pairs = [(i, target(i, step)) for i in range(UNITS)]
    return lax.ppermute(block, "sp", [(b, a) for a, b in pairs] if back else pairs)


def tables():
    sent = [{s: target(me, s) for s in STEPS[0] + STEPS[1]} for me in range(UNITS)]
    placed = []
    for me in range(UNITS):
        row = []
        for steps in STEPS:
            source = [next(i for i in range(UNITS) if target(i, s) == me) for s in steps]
            order = (0, 1, 2, 3) if me % 2 == 0 else (1, 2, 3, 0)
            for n in order:
                row += [n, source[n]]
        placed.append(row)
    return sent, placed


def all_to_all(array):
    return lax.all_to_all(array, "sp", split_axis=0, concat_axis=0, tiled=True)


def on_device(queries, grad_out, key_heads, value_heads, seq_start):
    even = lax.axis_index("dp") % 2 == 0
    window_first = lax.axis_index("dp") * BLK - PAST
    me = lax.axis_index("sp")
    by_head = lambda a: a.reshape(UNIT, HK, -1)
    sent, placed = tables()
    goes = {
        s: jnp.array([row[s] for row in sent], jnp.int32)[me] * HEADS * HD for s in sent[0]
    }
    part_of = lambda a, s: lax.dynamic_slice_in_dim(a, goes[s], HEADS * HD, 1)
    start = jnp.broadcast_to((seq_start[0] // UNIT).astype(BF), (HK, 16, 2 * HD))
    kv = jnp.concatenate([by_head(key_heads), by_head(value_heads)], axis=2).transpose(1, 0, 2)
    own = all_to_all(jnp.concatenate([kv, start], axis=1))
    units = {
        s: round_by(jnp.concatenate([part_of(queries, s), part_of(grad_out, s)], axis=1), s)
        for s in STEPS[0] + STEPS[1]
    }
    info = own[:, UNIT, 0].astype(F32).astype(jnp.int32) * UNIT - window_first
    info = jnp.concatenate([info, jnp.array(placed, jnp.int32)[me]])
    block = own[:, :UNIT].reshape(BLK, 2 * HD)
    h1 = shifted(block, 1)
    h3 = shifted(block, 3)
    near = [units[s] for s in STEPS[0]]
    h1, h3, *near = lax.optimization_barrier((h1, h3, *near))
    units.update(zip(STEPS[0], near))
    h2 = exchanged(jnp.where(even, h1, h3))
    grads, sums = {}, ()
    for last in (False, True):
        pieces = [units[s] for s in STEPS[last]]
        result = attend(last, info, pieces, (h3, h2, h1, block), sums)
        dq, sums = result[:4], result[4:]
        grads.update(zip(STEPS[last], dq))
    p3, p2, p1, mine = sums
    swap = exchanged(p2).astype(F32)
    t1 = (p1.astype(F32) + jnp.where(even, swap, 0.0)).astype(BF)
    t3 = (p3.astype(F32) + jnp.where(even, 0.0, swap)).astype(BF)
    order = sorted(grads, key=abs, reverse=True)
    t1, t3, *pieces = lax.optimization_barrier((t1, t3, *[grads[s] for s in order]))
    grads = {s: round_by(piece, s, True) for s, piece in zip(order, pieces)}
    total = mine + shifted(t1, -1).astype(F32) + shifted(t3, -3).astype(F32)
    dkv = all_to_all(total.astype(BF).reshape(UNITS, UNIT, 2 * HD)).transpose(1, 0, 2)
    query_grad = jnp.zeros((UNIT, HQ * HD), BF)
    for s, piece in grads.items():
        query_grad = lax.dynamic_update_slice_in_dim(query_grad, piece, goes[s], 1)
    key_grad = dkv[:, :, :HD].reshape(UNIT, HK * HD)
    value_grad = dkv[:, :, HD:].reshape(UNIT, HK * HD)
    return (query_grad, key_grad, value_grad)


def solution(mesh):
    rows = P(("dp", "sp"), None)
    return jax.shard_map(
        on_device,
        mesh=mesh,
        in_specs=(rows, rows, rows, rows, P(("dp", "sp"))),
        out_specs=(rows, rows, rows),
        check_vma=False,
    )
```
